32 devices in a mesh: groups: 2 (over x), view: 16 (over z, y, core).
Axes of the slice: x: 2, y: 2, z: 4, core: 2. Of those that a mesh axis runs over, the one named last changes fastest.
Arguments:
- query: bfloat16 [4096, 1024], P(('groups', 'view')), parts along dimension 0, may hold values from -28 to 28
- keys: bfloat16 [4096, 1024], P(('groups', 'view')), parts along dimension 0, may hold values from -6 to 6
- values: bfloat16 [4096, 1024], P(('groups', 'view')), parts along dimension 0, may hold values from -6 to 6
- grad_out: bfloat16 [4096, 1024], P(('groups', 'view')), parts along dimension 0, may hold values from -6 to 6
- margin: int32 [32, 4, 1, 1], P('groups'), parts along dimension 0, may hold values 0 or 1
Outputs:
- attended: bfloat16 [4096, 1024], P(('groups', 'view')), parts along dimension 0
- grad_query: bfloat16 [4096, 1024], P(('groups', 'view')), parts along dimension 0
- grad_key: bfloat16 [4096, 1024], P(('groups', 'view')), parts along dimension 0
- grad_value: bfloat16 [4096, 1024], P(('groups', 'view')), parts along dimension 0
The draws below stay inside these ranges and needn't reach their ends.
There are 2 independent parts, one for each index of `groups`. The reference program is written for one: setup_inputs(seed, part) draws one part's arguments, and reference() takes and returns one part's arrays. A program takes and returns all parts, laid end to end along the dimension named above; each array names one. Nothing has to cross between parts.
All inputs are finite; a program needn't handle non-finite values.
Results may differ from the reference program's by a relative error of at most 0.033.
Values may be sent and summed in bfloat16 or wider, within the bound.
A program may use at most 64 MiB of HBM per device.

```python
import math
import jax
import jax.numpy as jnp
from jax import lax

H = 8
DH = 128
HW = 1024
IMG_TOK = 128
BLK = 128
NB = 1
SPAN = 2
IMAGES = 16
ROWS = 2048


def drawn_pair(key):
    base = jax.random.fold_in(key, 7)
    first, second = jax.random.split(base, 2)
    shape = (IMAGES, IMG_TOK, HW)
    query_draw = jax.random.truncated_normal(first, -6.0, 6.0, shape, jnp.float32)
    key_draw = jax.random.truncated_normal(second, -6.0, 6.0, shape, jnp.float32)
    return (query_draw.reshape(ROWS, HW), key_draw.reshape(ROWS, HW))


def draw_query(key, part):
    return drawn_pair(key)[0].astype(jnp.bfloat16)


def draw_keys(key, part):
    return drawn_pair(key)[1].astype(jnp.bfloat16)


def plant(drawn, key, least, high):
    dims = drawn.shape
    place = [jax.random.randint(jax.random.fold_in(key, axis), (), 0, dims[axis]) for axis in range(len(dims))]
    drawn = drawn.at[tuple(place)].set(least)
    longest = dims.index(max(dims))
    place[longest] = (place[longest] + 1) % dims[longest]
    return drawn.at[tuple(place)].set(high)


def block_scale(key, shape, shards, least, top_value):
    loudness, own = 1.0, jax.random.fold_in(key, 6)
    for position, blocks in shards:
        heights = jnp.exp(jax.random.uniform(jax.random.fold_in(own, position), (blocks,), jnp.float32, least / len(shards), top_value / len(shards)))
        loudness = loudness * jnp.repeat(heights, shape[position] // blocks).reshape([-1 if axis == position else 1 for axis in range(len(shape))])
    return loudness


def bell_draw(key, shape, width, limit, shards=(), held_as=jnp.bfloat16):
    entries = width * jax.random.normal(key, shape, jnp.float32)
    if shards:
        entries = entries * block_scale(key, shape, shards, -0.22, 0.18)
    return jnp.clip(entries, -limit, limit).astype(held_as)


def setup_inputs(seed: int = 0, part: int = 0) -> dict:
    key_of = jax.random.split(jax.random.key(seed), 6)
    part_keys = jax.random.split(jax.random.fold_in(key_of[5], part), 6)
    query = draw_query(jax.random.fold_in(jax.random.fold_in(key_of[5], part), 71), part)
    keys = draw_keys(jax.random.fold_in(jax.random.fold_in(key_of[5], part), 71), part)
    values = bell_draw(part_keys[2], (ROWS, HW), 1.0, 6.0, ((0, 16),))
    grad_out = bell_draw(part_keys[3], (ROWS, HW), 1.0, 6.0, ((0, 16),))
    margin = plant((jax.random.randint(part_keys[4], (IMAGES, 2 * SPAN, NB, NB), 0, 3) < 1).astype(jnp.int32), jax.random.fold_in(part_keys[4], 1), 0, 1)
    return {"query": query, "keys": keys, "values": values, "grad_out": grad_out, "margin": margin}


NEG_FILL = -1e+30

def allowed_grid(margin, image_index):
    mask_row = lax.dynamic_index_in_dim(margin, image_index, 0, keepdims=False)
    filled = jnp.ones((1, NB, NB), mask_row.dtype)
    mask_spans = jnp.concatenate([mask_row[:SPAN], filled, mask_row[SPAN:]], axis=0)
    block_grid = jnp.transpose(mask_spans, (1, 0, 2)).reshape(NB, (2 * SPAN + 1) * NB)
    return jnp.repeat(jnp.repeat(block_grid, BLK, axis=0), BLK, axis=1) > 0

def reference(query, keys, values, grad_out, margin):
    query_images = query.reshape(IMAGES, IMG_TOK, H, DH)
    key_images = keys.reshape(IMAGES, IMG_TOK, H, DH)
    value_images = values.reshape(IMAGES, IMG_TOK, H, DH)
    grad_images = grad_out.reshape(IMAGES, IMG_TOK, H, DH)
    score_scale = 1.0 / math.sqrt(DH)
    shifts = jnp.arange(-SPAN, SPAN + 1, dtype=jnp.int32)

    def visit(running, image_index):
        key_acc, value_acc = running
        neighbours = ((image_index + shifts) % IMAGES).astype(jnp.int32)
        key_all = jnp.take(key_images, neighbours, axis=0).reshape(-1, H, DH).astype(jnp.float32)
        value_all = jnp.take(value_images, neighbours, axis=0).reshape(-1, H, DH).astype(jnp.float32)
        query_here = lax.dynamic_index_in_dim(query_images, image_index, 0, keepdims=False).astype(jnp.float32)
        grad_here = lax.dynamic_index_in_dim(grad_images, image_index, 0, keepdims=False).astype(jnp.float32)
        allowed = allowed_grid(margin, image_index)
        scores = jnp.einsum('qhd,khd->hqk', query_here, key_all) * score_scale
        scores = jnp.where(allowed[None], scores, NEG_FILL)
        row_max = lax.optimization_barrier(jnp.max(scores, axis=-1, keepdims=True))
        log_total = row_max + jnp.log(lax.optimization_barrier(jnp.sum(jnp.exp(scores - row_max), axis=-1, keepdims=True)))
        prob_full = jnp.exp(scores - log_total)
        prob_half = lax.optimization_barrier(prob_full.astype(jnp.bfloat16)).astype(jnp.float32)
        attended = jnp.einsum('hqk,khd->qhd', prob_half, value_all).astype(jnp.bfloat16)
        row_dot = lax.optimization_barrier(jnp.sum(grad_here * attended.astype(jnp.float32), axis=-1))
        row_dot = jnp.transpose(row_dot)[..., None]
        prob_grad = jnp.einsum('qhd,khd->hqk', grad_here, value_all)
        grad_half = lax.optimization_barrier((prob_full * (prob_grad - row_dot)).astype(jnp.bfloat16)).astype(jnp.float32)
        grad_query = (jnp.einsum('hqk,khd->qhd', grad_half, key_all) * score_scale).astype(jnp.bfloat16)
        key_terms = jnp.einsum('hqk,qhd->khd', grad_half, query_here).reshape(2 * SPAN + 1, IMG_TOK, H, DH)
        value_terms = jnp.einsum('hqk,qhd->khd', prob_half, grad_here).reshape(2 * SPAN + 1, IMG_TOK, H, DH)
        for pair_index in range(2 * SPAN + 1):
            target = neighbours[pair_index]
            key_acc = key_acc.at[target].add(key_terms[pair_index])
            value_acc = value_acc.at[target].add(value_terms[pair_index])
        return ((key_acc, value_acc), (attended, grad_query))
    empty = jnp.zeros((IMAGES, IMG_TOK, H, DH), jnp.float32)
    (key_acc, value_acc), (attended, grad_query) = lax.scan(visit, (empty, empty), jnp.arange(IMAGES, dtype=jnp.int32))
    grad_key = (key_acc * score_scale).astype(jnp.bfloat16).reshape(ROWS, HW)
    grad_value = value_acc.astype(jnp.bfloat16).reshape(ROWS, HW)
    return (attended.reshape(ROWS, HW), grad_query.reshape(ROWS, HW), grad_key, grad_value)
```

```python
import functools
import math

import jax
import jax.numpy as jnp
from jax import lax
from jax.experimental import pallas as pl
from jax.experimental.pallas import tpu as pltpu
from jax.sharding import PartitionSpec as P

H = 8
SPAN = 2
NEG_FILL = -1e30

PARTNER, RELAY, SIBLING, PASSED, OWN = range(5)
BLOCKS = 2 * SPAN + 1


def kernel(
    devices,
    q_ref,
    k_ref,
    v_ref,
    do_ref,
    margin_ref,
    att_ref,
    gq_ref,
    gk_ref,
    gv_ref,
    kv,
    acc,
    bias,
    out_buf,
    in_buf,
    kv_send,
    kv_recv,
    pass_send,
    g_send,
    g_recv,
):
    tokens, width = q_ref.shape
    dim = width // H
    scale = 1.0 / math.sqrt(dim)
    me = lax.axis_index("view")
    core = lax.rem(me, 2)
    chip = me // 2
    odd = lax.rem(chip, 2)
    sign = 1 - 2 * odd
    sibling = me + 1 - 2 * core
    partner = me + 2 * sign
    onward = lax.rem(me + 4 * sign + devices, devices)
    source = lax.rem(me - 4 * sign + devices, devices)
    shared = lax.rem(odd + core, 2)

    def cols(h):
        return pl.ds(pl.multiple_of(h * dim, dim), dim)

    def rows(block):
        return pl.ds(block * tokens, tokens)

    def send(src, dst, send_sem, recv_sem, to):
        return pltpu.make_async_remote_copy(
            src_ref=src,
            dst_ref=dst,
            send_sem=send_sem,
            recv_sem=recv_sem,
            device_id={"view": to},
            device_id_type=pl.DeviceIdType.MESH,
        )

    def first(h, block, part, to):
        return send(
            (k_ref, v_ref)[part].at[:, cols(h)],
            kv.at[h, part, rows(block), :],
            kv_send.at[block, part, h],
            kv_recv.at[block, part, h],
            to,
        )

    def relay(h):
        return send(
            kv.at[h, :, rows(PARTNER), :],
            kv.at[h, :, rows(RELAY), :],
            pass_send.at[0, h],
            kv_recv.at[RELAY, 0, h],
            onward,
        )

    def forward(h, block):
        return send(
            kv.at[h, :, rows(block), :],
            kv.at[h, :, rows(PASSED), :],
            pass_send.at[1, h],
            kv_recv.at[PASSED, 0, h],
            sibling,
        )

    def grad(h, block, to):
        return send(
            out_buf.at[h, block],
            in_buf.at[h, block],
            g_send.at[block, h],
            g_recv.at[block, h],
            to,
        )

    barrier = pltpu.get_barrier_semaphore()
    for peer in (sibling, partner, onward, source):
        pl.semaphore_signal(
            barrier, inc=1, device_id={"view": peer}, device_id_type=pl.DeviceIdType.MESH
        )
    pl.semaphore_wait(barrier, 4)

    @pl.loop(0, H)
    def _(h):
        for part in range(2):
            first(h, PARTNER, part, partner).start()
        for part in range(2):
            first(h, SIBLING, part, sibling).start()

    side = 1 - 2 * core
    order = (2 * sign, -2 * sign, side, -side)
    for block, offset in enumerate(order):
        place = offset + SPAN - (offset + SPAN) // (SPAN + 1)
        mask = margin_ref[me, place].astype(jnp.float32)
        bias[:, block * tokens : (block + 1) * tokens] = jnp.full(
            (8, tokens), (1.0 - mask) * NEG_FILL, jnp.float32
        )
    bias[:, OWN * tokens :] = jnp.zeros((8, tokens), jnp.float32)
    for h in range(H):
        kv[h, 0, OWN * tokens :, :] = k_ref[:, h * dim : (h + 1) * dim]
        kv[h, 1, OWN * tokens :, :] = v_ref[:, h * dim : (h + 1) * dim]

    def dot(a, b, ca, cb):
        return lax.dot_general(a, b, (((ca,), (cb,)), ((), ())), preferred_element_type=jnp.float32)

    def compute(h):
        q = q_ref[:, cols(h)]
        do = do_ref[:, cols(h)]
        k_all = kv[h, 0]
        v_all = kv[h, 1]
        scores = dot(q, k_all, 1, 1) * scale + bias[0:1, :]
        e = jnp.exp(scores - jnp.max(scores, axis=-1, keepdims=True))
        prob = e * (1.0 / jnp.sum(e, axis=-1, keepdims=True))
        prob_half = prob.astype(jnp.bfloat16)
        att = dot(prob_half, v_all, 1, 0).astype(jnp.bfloat16)
        att_ref[:, cols(h)] = att
        row_dot = jnp.sum(
            do.astype(jnp.float32) * att.astype(jnp.float32), axis=-1, keepdims=True
        )
        prob_grad = dot(do, v_all, 1, 1)
        grad_half = (prob * (prob_grad - row_dot)).astype(jnp.bfloat16)
        gq_ref[:, cols(h)] = (dot(grad_half, k_all, 1, 0) * scale).astype(jnp.bfloat16)
        acc[h, 0] = dot(grad_half, q, 0, 0)
        acc[h, 1] = dot(prob_half, do, 0, 0)

    @pl.loop(0, H + 5)
    def _(t):
        @pl.when(t < H)
        def _():
            for part in range(2):
                first(t, PARTNER, part, partner).wait_recv()
            relay(t).start()

            @pl.when(shared == PARTNER)
            def _():
                forward(t, PARTNER).start()

        @pl.when((t >= 1) & (t < H + 1))
        def _():
            h = t - 1
            relay(h).wait_recv()

            @pl.when(shared == RELAY)
            def _():
                forward(h, RELAY).start()

        @pl.when((t >= 2) & (t < H + 2))
        def _():
            h = t - 2
            for part in range(2):
                first(h, SIBLING, part, sibling).wait_recv()
            forward(h, PARTNER).wait_recv()
            compute(h)
            for block in (PASSED, SIBLING):
                out_buf[h, block] = acc[h, :, block * tokens : (block + 1) * tokens, :].astype(
                    jnp.bfloat16
                )
                grad(h, block, sibling).start()

        @pl.when((t >= 3) & (t < H + 3))
        def _():
            h = t - 3
            grad(h, PASSED, sibling).wait_recv()
            place = pl.ds(pl.multiple_of(shared * tokens, tokens), tokens)
            acc[h, :, place, :] += in_buf[h, PASSED].astype(jnp.float32)
            out_buf[h, RELAY] = acc[h, :, RELAY * tokens : (RELAY + 1) * tokens, :].astype(
                jnp.bfloat16
            )
            grad(h, RELAY, source).start()

        @pl.when((t >= 4) & (t < H + 4))
        def _():
            h = t - 4
            grad(h, RELAY, source).wait_recv()
            out_buf[h, PARTNER] = (
                acc[h, :, :tokens, :] + in_buf[h, RELAY].astype(jnp.float32)
            ).astype(jnp.bfloat16)
            grad(h, PARTNER, partner).start()

        @pl.when(t >= 5)
        def _():
            h = t - 5
            grad(h, SIBLING, sibling).wait_recv()
            grad(h, PARTNER, partner).wait_recv()
            total = (
                acc[h, :, OWN * tokens :, :]
                + in_buf[h, SIBLING].astype(jnp.float32)
                + in_buf[h, PARTNER].astype(jnp.float32)
            )
            gk_ref[:, cols(h)] = (total[0] * scale).astype(jnp.bfloat16)
            gv_ref[:, cols(h)] = total[1].astype(jnp.bfloat16)

    @pl.loop(0, H)
    def _(h):
        for part in range(2):
            first(h, PARTNER, part, partner).wait_send()
            first(h, SIBLING, part, sibling).wait_send()
        relay(h).wait_send()
        forward(h, PARTNER).wait_send()
        grad(h, PASSED, sibling).wait_send()
        grad(h, SIBLING, sibling).wait_send()
        grad(h, RELAY, source).wait_send()
        grad(h, PARTNER, partner).wait_send()


def body(devices, query, keys, values, grad_out, margin):
    tokens, width = query.shape
    dim = width // H
    vmem = pl.BlockSpec(memory_space=pltpu.VMEM)
    shape = jax.ShapeDtypeStruct((tokens, width), jnp.bfloat16)
    dma = pltpu.SemaphoreType.DMA
    return pl.pallas_call(
        functools.partial(kernel, devices),
        out_shape=(shape,) * 4,
        in_specs=[vmem] * 4 + [pl.BlockSpec(memory_space=pltpu.SMEM)],
        out_specs=(vmem,) * 4,
        scratch_shapes=[
            pltpu.VMEM((H, 2, BLOCKS * tokens, dim), jnp.bfloat16),
            pltpu.VMEM((H, 2, BLOCKS * tokens, dim), jnp.float32),
            pltpu.VMEM((8, BLOCKS * tokens), jnp.float32),
            pltpu.VMEM((H, 4, 2, tokens, dim), jnp.bfloat16),
            pltpu.VMEM((H, 4, 2, tokens, dim), jnp.bfloat16),
            dma((4, 2, H)),
            dma((4, 2, H)),
            dma((2, H)),
            dma((4, H)),
            dma((4, H)),
        ],
        compiler_params=pltpu.CompilerParams(
            collective_id=0, has_side_effects=True, vmem_limit_bytes=40 * 1024 * 1024
        ),
    )(query, keys, values, grad_out, margin.reshape(margin.shape[:2]))


def solution(mesh):
    split = P(("groups", "view"), None)
    return jax.shard_map(
        functools.partial(body, mesh.shape["view"]),
        mesh=mesh,
        in_specs=(split,) * 4 + (P("groups", None, None, None),),
        out_specs=(split,) * 4,
        check_vma=False,
    )
```

```python
import functools
import math

import jax
import jax.numpy as jnp
from jax import lax
from jax.experimental import pallas as pl
from jax.experimental.pallas import tpu as pltpu
from jax.sharding import PartitionSpec as P

H = 8
SPAN = 2
NEG_FILL = -1e30

PARTNER, RELAY, SIBLING, PASSED, OWN = range(5)
BLOCKS = 2 * SPAN + 1

AHEAD = 4

RELAYED, READY, SUMMED, RETURNED, DONE = 3, 4, 5, 8, 11


def kernel(
    devices,
    q_ref,
    k_ref,
    v_ref,
    do_ref,
    margin_ref,
    att_ref,
    gq_ref,
    gk_ref,
    gv_ref,
    kv,
    acc,
    bias,
    out_buf,
    in_buf,
    kv_send,
    kv_recv,
    pass_send,
    g_send,
    g_recv,
):
    tokens, width = q_ref.shape
    dim = width // H
    scale = 1.0 / math.sqrt(dim)
    me = lax.axis_index("view")
    core = lax.rem(me, 2)
    chip = me // 2
    odd = lax.rem(chip, 2)
    sign = 1 - 2 * odd
    sibling = me + 1 - 2 * core
    partner = me + 2 * sign
    onward = lax.rem(me + 4 * sign + devices, devices)
    source = lax.rem(me - 4 * sign + devices, devices)
    shared = lax.rem(odd + core, 2)

    def cols(h):
        return pl.ds(pl.multiple_of(h * dim, dim), dim)

    def rows(block):
        return pl.ds(block * tokens, tokens)

    def send(src, dst, send_sem, recv_sem, to):
        return pltpu.make_async_remote_copy(
            src_ref=src,
            dst_ref=dst,
            send_sem=send_sem,
            recv_sem=recv_sem,
            device_id={"view": to},
            device_id_type=pl.DeviceIdType.MESH,
        )

    def first(h, block, part, to):
        return send(
            (k_ref, v_ref)[part].at[:, cols(h)],
            kv.at[h, part, rows(block), :],
            kv_send.at[block, part, h],
            kv_recv.at[block, part, h],
            to,
        )

    def relay(h):
        return send(
            kv.at[h, :, rows(PARTNER), :],
            kv.at[h, :, rows(RELAY), :],
            pass_send.at[0, h],
            kv_recv.at[RELAY, 0, h],
            onward,
        )

    def forward(h, block):
        return send(
            kv.at[h, :, rows(block), :],
            kv.at[h, :, rows(PASSED), :],
            pass_send.at[1, h],
            kv_recv.at[PASSED, 0, h],
            sibling,
        )

    def grad(h, block, to):
        return send(
            out_buf.at[h, block],
            in_buf.at[h, block],
            g_send.at[block, h],
            g_recv.at[block, h],
            to,
        )

    barrier = pltpu.get_barrier_semaphore()
    for peer in (sibling, partner, onward, source):
        pl.semaphore_signal(
            barrier, inc=1, device_id={"view": peer}, device_id_type=pl.DeviceIdType.MESH
        )
    pl.semaphore_wait(barrier, 4)

    def launch(h):
        for part in range(2):
            first(h, PARTNER, part, partner).start()
        for part in range(2):
            first(h, SIBLING, part, sibling).start()

    for h in range(AHEAD):
        launch(h)

    side = 1 - 2 * core
    order = (2 * sign, -2 * sign, side, -side)
    for block, offset in enumerate(order):
        place = offset + SPAN - (offset + SPAN) // (SPAN + 1)
        mask = margin_ref[me, place].astype(jnp.float32)
        bias[:, block * tokens : (block + 1) * tokens] = jnp.full(
            (8, tokens), (1.0 - mask) * NEG_FILL, jnp.float32
        )
    bias[:, OWN * tokens :] = jnp.zeros((8, tokens), jnp.float32)
    for h in range(H):
        kv[h, 0, OWN * tokens :, :] = k_ref[:, h * dim : (h + 1) * dim]
        kv[h, 1, OWN * tokens :, :] = v_ref[:, h * dim : (h + 1) * dim]

    def dot(a, b, ca, cb):
        return lax.dot_general(a, b, (((ca,), (cb,)), ((), ())), preferred_element_type=jnp.float32)

    def compute(h):
        q = q_ref[:, cols(h)]
        do = do_ref[:, cols(h)]
        k_all = kv[h, 0]
        v_all = kv[h, 1]
        scores = dot(q, k_all, 1, 1) * scale + bias[0:1, :]
        e = jnp.exp(scores - jnp.max(scores, axis=-1, keepdims=True))
        prob = e * (1.0 / jnp.sum(e, axis=-1, keepdims=True))
        prob_half = prob.astype(jnp.bfloat16)
        att = dot(prob_half, v_all, 1, 0).astype(jnp.bfloat16)
        att_ref[:, cols(h)] = att
        row_dot = jnp.sum(
            do.astype(jnp.float32) * att.astype(jnp.float32), axis=-1, keepdims=True
        )
        prob_grad = dot(do, v_all, 1, 1)
        grad_half = (prob * (prob_grad - row_dot)).astype(jnp.bfloat16)
        gq_ref[:, cols(h)] = (dot(grad_half, k_all, 1, 0) * scale).astype(jnp.bfloat16)
        acc[h, 0] = dot(grad_half, q, 0, 0)
        acc[h, 1] = dot(prob_half, do, 0, 0)

    @pl.loop(0, H + DONE)
    def _(t):
        @pl.when(t < H)
        def _():
            for part in range(2):
                first(t, PARTNER, part, partner).wait_recv()
            relay(t).start()

            @pl.when(t + AHEAD < H)
            def _():
                launch(t + AHEAD)

            @pl.when(shared == PARTNER)
            def _():
                forward(t, PARTNER).start()

        @pl.when((t >= RELAYED) & (t < H + RELAYED))
        def _():
            h = t - RELAYED
            relay(h).wait_recv()

            @pl.when(shared == RELAY)
            def _():
                forward(h, RELAY).start()

        @pl.when((t >= READY) & (t < H + READY))
        def _():
            h = t - READY
            for part in range(2):
                first(h, SIBLING, part, sibling).wait_recv()
            forward(h, PARTNER).wait_recv()
            compute(h)
            for block in (PASSED, SIBLING):
                out_buf[h, block] = acc[h, :, block * tokens : (block + 1) * tokens, :].astype(
                    jnp.bfloat16
                )
                grad(h, block, sibling).start()

        @pl.when((t >= SUMMED) & (t < H + SUMMED))
        def _():
            h = t - SUMMED
            grad(h, PASSED, sibling).wait_recv()
            place = pl.ds(pl.multiple_of(shared * tokens, tokens), tokens)
            acc[h, :, place, :] += in_buf[h, PASSED].astype(jnp.float32)
            out_buf[h, RELAY] = acc[h, :, RELAY * tokens : (RELAY + 1) * tokens, :].astype(
                jnp.bfloat16
            )
            grad(h, RELAY, source).start()

        @pl.when((t >= RETURNED) & (t < H + RETURNED))
        def _():
            h = t - RETURNED
            grad(h, RELAY, source).wait_recv()
            out_buf[h, PARTNER] = (
                acc[h, :, :tokens, :] + in_buf[h, RELAY].astype(jnp.float32)
            ).astype(jnp.bfloat16)
            grad(h, PARTNER, partner).start()

        @pl.when(t >= DONE)
        def _():
            h = t - DONE
            grad(h, SIBLING, sibling).wait_recv()
            grad(h, PARTNER, partner).wait_recv()
            total = (
                acc[h, :, OWN * tokens :, :]
                + in_buf[h, SIBLING].astype(jnp.float32)
                + in_buf[h, PARTNER].astype(jnp.float32)
            )
            gk_ref[:, cols(h)] = (total[0] * scale).astype(jnp.bfloat16)
            gv_ref[:, cols(h)] = total[1].astype(jnp.bfloat16)

    @pl.loop(0, H)
    def _(h):
        for part in range(2):
            first(h, PARTNER, part, partner).wait_send()
            first(h, SIBLING, part, sibling).wait_send()
        relay(h).wait_send()
        forward(h, PARTNER).wait_send()
        grad(h, PASSED, sibling).wait_send()
        grad(h, SIBLING, sibling).wait_send()
        grad(h, RELAY, source).wait_send()
        grad(h, PARTNER, partner).wait_send()


def body(devices, query, keys, values, grad_out, margin):
    tokens, width = query.shape
    dim = width // H
    vmem = pl.BlockSpec(memory_space=pltpu.VMEM)
    shape = jax.ShapeDtypeStruct((tokens, width), jnp.bfloat16)
    dma = pltpu.SemaphoreType.DMA
    return pl.pallas_call(
        functools.partial(kernel, devices),
        out_shape=(shape,) * 4,
        in_specs=[vmem] * 4 + [pl.BlockSpec(memory_space=pltpu.SMEM)],
        out_specs=(vmem,) * 4,
        scratch_shapes=[
            pltpu.VMEM((H, 2, BLOCKS * tokens, dim), jnp.bfloat16),
            pltpu.VMEM((H, 2, BLOCKS * tokens, dim), jnp.float32),
            pltpu.VMEM((8, BLOCKS * tokens), jnp.float32),
            pltpu.VMEM((H, 4, 2, tokens, dim), jnp.bfloat16),
            pltpu.VMEM((H, 4, 2, tokens, dim), jnp.bfloat16),
            dma((4, 2, H)),
            dma((4, 2, H)),
            dma((2, H)),
            dma((4, H)),
            dma((4, H)),
        ],
        compiler_params=pltpu.CompilerParams(
            collective_id=0, has_side_effects=True, vmem_limit_bytes=40 * 1024 * 1024
        ),
    )(query, keys, values, grad_out, margin.reshape(margin.shape[:2]))


def solution(mesh):
    split = P(("groups", "view"), None)
    return jax.shard_map(
        functools.partial(body, mesh.shape["view"]),
        mesh=mesh,
        in_specs=(split,) * 4 + (P("groups", None, None, None),),
        out_specs=(split,) * 4,
        check_vma=False,
    )
```

```python
import functools
import math

import jax
import jax.numpy as jnp
from jax import lax
from jax.experimental import pallas as pl
from jax.experimental.pallas import tpu as pltpu
from jax.sharding import PartitionSpec as P

H = 8
SPAN = 2
NEG_FILL = -1e30

PARTNER, RELAY, SIBLING, PASSED, OWN = range(5)
BLOCKS = 2 * SPAN + 1
VMEM_LIMIT = 60 * 1024 * 1024

AHEAD = 4

RELAYED, READY, SUMMED, RETURNED, DONE = 3, 4, 5, 8, 11


def kernel(
    devices,
    q_hbm,
    k_hbm,
    v_hbm,
    do_hbm,
    margin_ref,
    att_hbm,
    gq_hbm,
    gk_hbm,
    gv_hbm,
    q_ref,
    do_ref,
    att_ref,
    gq_ref,
    gk_ref,
    gv_ref,
    kv,
    acc,
    bias,
    out_buf,
    in_buf,
    load_sem,
    store_sem,
    kv_load,
    kv_send,
    kv_recv,
    pass_send,
    g_send,
    g_recv,
):
    tokens, width = q_hbm.shape
    dim = width // H
    scale = 1.0 / math.sqrt(dim)
    me = lax.axis_index("view")
    core = lax.rem(me, 2)
    chip = me // 2
    odd = lax.rem(chip, 2)
    sign = 1 - 2 * odd
    sibling = me + 1 - 2 * core
    partner = me + 2 * sign
    onward = lax.rem(me + 4 * sign + devices, devices)
    source = lax.rem(me - 4 * sign + devices, devices)
    shared = lax.rem(odd + core, 2)

    def cols(h):
        return pl.ds(pl.multiple_of(h * dim, dim), dim)

    def rows(block):
        return pl.ds(block * tokens, tokens)

    def send(src, dst, send_sem, recv_sem, to):
        return pltpu.make_async_remote_copy(
            src_ref=src,
            dst_ref=dst,
            send_sem=send_sem,
            recv_sem=recv_sem,
            device_id={"view": to},
            device_id_type=pl.DeviceIdType.MESH,
        )

    def load(h, part):
        return pltpu.make_async_copy(
            (k_hbm, v_hbm)[part].at[:, cols(h)], kv.at[h, part, rows(OWN), :], kv_load.at[part, h]
        )

    def store(h, n):
        return pltpu.make_async_copy(
            (att_ref, gq_ref, gk_ref, gv_ref)[n].at[:, cols(h)],
            (att_hbm, gq_hbm, gk_hbm, gv_hbm)[n].at[:, cols(h)],
            store_sem.at[n, h],
        )

    def first(h, block, to):
        return send(
            kv.at[h, :, rows(OWN), :],
            kv.at[h, :, rows(block), :],
            kv_send.at[block, h],
            kv_recv.at[block, h],
            to,
        )

    def relay(h):
        return send(
            kv.at[h, :, rows(PARTNER), :],
            kv.at[h, :, rows(RELAY), :],
            pass_send.at[0, h],
            kv_recv.at[RELAY, h],
            onward,
        )

    def forward(h, block):
        return send(
            kv.at[h, :, rows(block), :],
            kv.at[h, :, rows(PASSED), :],
            pass_send.at[1, h],
            kv_recv.at[PASSED, h],
            sibling,
        )

    def grad(h, block, to):
        return send(
            out_buf.at[h, block],
            in_buf.at[h, block],
            g_send.at[block, h],
            g_recv.at[block, h],
            to,
        )

    loads = (
        pltpu.make_async_copy(q_hbm, q_ref, load_sem.at[0]),
        pltpu.make_async_copy(do_hbm, do_ref, load_sem.at[1]),
    )
    barrier = pltpu.get_barrier_semaphore()
    for peer in (sibling, partner, onward, source):
        pl.semaphore_signal(
            barrier, inc=1, device_id={"view": peer}, device_id_type=pl.DeviceIdType.MESH
        )
    for h in range(H):
        for part in range(2):
            load(h, part).start()
    for copy in loads:
        copy.start()
    side = 1 - 2 * core
    order = (2 * sign, -2 * sign, side, -side)
    for block, offset in enumerate(order):
        place = offset + SPAN - (offset + SPAN) // (SPAN + 1)
        mask = margin_ref[place, me].astype(jnp.float32)
        bias[:, block * tokens : (block + 1) * tokens] = jnp.full(
            (8, tokens), (1.0 - mask) * NEG_FILL, jnp.float32
        )
    bias[:, OWN * tokens :] = jnp.zeros((8, tokens), jnp.float32)
    pl.semaphore_wait(barrier, 4)

    def launch(h):
        for part in range(2):
            load(h, part).wait()
        first(h, PARTNER, partner).start()
        first(h, SIBLING, sibling).start()

    for h in range(AHEAD):
        launch(h)
    for copy in loads:
        copy.wait()

    def dot(a, b, ca, cb):
        return lax.dot_general(a, b, (((ca,), (cb,)), ((), ())), preferred_element_type=jnp.float32)

    def compute(h):
        q = q_ref[:, cols(h)]
        do = do_ref[:, cols(h)]
        k_all = kv[h, 0]
        v_all = kv[h, 1]
        scores = dot(q, k_all, 1, 1) * scale + bias[0:1, :]
        e = jnp.exp(scores - jnp.max(scores, axis=-1, keepdims=True))
        prob = e * (1.0 / jnp.sum(e, axis=-1, keepdims=True))
        prob_half = prob.astype(jnp.bfloat16)
        att = dot(prob_half, v_all, 1, 0).astype(jnp.bfloat16)
        att_ref[:, cols(h)] = att
        row_dot = jnp.sum(
            do.astype(jnp.float32) * att.astype(jnp.float32), axis=-1, keepdims=True
        )
        prob_grad = dot(do, v_all, 1, 1)
        grad_half = (prob * (prob_grad - row_dot)).astype(jnp.bfloat16)
        gq_ref[:, cols(h)] = (dot(grad_half, k_all, 1, 0) * scale).astype(jnp.bfloat16)
        acc[h, 0] = dot(grad_half, q, 0, 0)
        acc[h, 1] = dot(prob_half, do, 0, 0)

    @pl.loop(0, H + DONE)
    def _(t):
        @pl.when(t < H)
        def _():
            first(t, PARTNER, partner).wait_recv()
            relay(t).start()

            @pl.when(t + AHEAD < H)
            def _():
                launch(t + AHEAD)

            @pl.when(shared == PARTNER)
            def _():
                forward(t, PARTNER).start()

        @pl.when((t >= RELAYED) & (t < H + RELAYED))
        def _():
            h = t - RELAYED
            relay(h).wait_recv()

            @pl.when(shared == RELAY)
            def _():
                forward(h, RELAY).start()

        @pl.when((t >= READY) & (t < H + READY))
        def _():
            h = t - READY
            first(h, SIBLING, sibling).wait_recv()
            forward(h, PARTNER).wait_recv()
            compute(h)
            for block in (PASSED, SIBLING):
                out_buf[h, block] = acc[h, :, block * tokens : (block + 1) * tokens, :].astype(
                    jnp.bfloat16
                )
                grad(h, block, sibling).start()
            store(h, 0).start()
            store(h, 1).start()

        @pl.when((t >= SUMMED) & (t < H + SUMMED))
        def _():
            h = t - SUMMED
            grad(h, PASSED, sibling).wait_recv()
            place = pl.ds(pl.multiple_of(shared * tokens, tokens), tokens)
            acc[h, :, place, :] += in_buf[h, PASSED].astype(jnp.float32)
            out_buf[h, RELAY] = acc[h, :, RELAY * tokens : (RELAY + 1) * tokens, :].astype(
                jnp.bfloat16
            )
            grad(h, RELAY, source).start()

        @pl.when((t >= RETURNED) & (t < H + RETURNED))
        def _():
            h = t - RETURNED
            grad(h, RELAY, source).wait_recv()
            out_buf[h, PARTNER] = (
                acc[h, :, :tokens, :] + in_buf[h, RELAY].astype(jnp.float32)
            ).astype(jnp.bfloat16)
            grad(h, PARTNER, partner).start()

        @pl.when(t >= DONE)
        def _():
            h = t - DONE
            grad(h, SIBLING, sibling).wait_recv()
            grad(h, PARTNER, partner).wait_recv()
            total = (
                acc[h, :, OWN * tokens :, :]
                + in_buf[h, SIBLING].astype(jnp.float32)
                + in_buf[h, PARTNER].astype(jnp.float32)
            )
            gk_ref[:, cols(h)] = (total[0] * scale).astype(jnp.bfloat16)
            gv_ref[:, cols(h)] = total[1].astype(jnp.bfloat16)
            store(h, 2).start()
            store(h, 3).start()

    @pl.loop(0, H)
    def _(h):
        first(h, PARTNER, partner).wait_send()
        first(h, SIBLING, sibling).wait_send()
        relay(h).wait_send()
        forward(h, PARTNER).wait_send()
        grad(h, PASSED, sibling).wait_send()
        grad(h, SIBLING, sibling).wait_send()
        grad(h, RELAY, source).wait_send()
        grad(h, PARTNER, partner).wait_send()
        for n in range(4):
            store(h, n).wait()


def store_kernel(*refs):
    sources, targets, held, sem = refs[:4], refs[4:8], refs[8], refs[9]
    fetches = [
        pltpu.make_async_copy(sources[n], held.at[n], sem.at[0, n]) for n in range(4)
    ]
    stores = [
        pltpu.make_async_copy(held.at[n], targets[n], sem.at[1, n]) for n in range(4)
    ]
    for fetch in fetches:
        fetch.start()
    for fetch, store in zip(fetches, stores):
        fetch.wait()
        store.start()
    for store in stores:
        store.wait()


def body(devices, query, keys, values, grad_out, margin):
    tokens, width = query.shape
    dim = width // H
    hbm = pl.BlockSpec(memory_space=pltpu.HBM)
    shape = jax.ShapeDtypeStruct((tokens, width), jnp.bfloat16)
    dma = pltpu.SemaphoreType.DMA
    results = pl.pallas_call(
        functools.partial(kernel, devices),
        out_shape=(shape,) * 4,
        in_specs=[hbm] * 4 + [pl.BlockSpec(memory_space=pltpu.SMEM)],
        out_specs=(hbm,) * 4,
        scratch_shapes=[
            *[pltpu.VMEM((tokens, width), jnp.bfloat16)] * 6,
            pltpu.VMEM((H, 2, BLOCKS * tokens, dim), jnp.bfloat16),
            pltpu.VMEM((H, 2, BLOCKS * tokens, dim), jnp.float32),
            pltpu.VMEM((8, BLOCKS * tokens), jnp.float32),
            pltpu.VMEM((H, 4, 2, tokens, dim), jnp.bfloat16),
            pltpu.VMEM((H, 4, 2, tokens, dim), jnp.bfloat16),
            dma((2,)),
            dma((4, H)),
            dma((2, H)),
            dma((4, H)),
            dma((4, H)),
            dma((2, H)),
            dma((4, H)),
            dma((4, H)),
        ],
        compiler_params=pltpu.CompilerParams(
            collective_id=0, has_side_effects=True, vmem_limit_bytes=VMEM_LIMIT
        ),
    )(query, keys, values, grad_out, margin.reshape(margin.shape[:2]).T)
    return pl.pallas_call(
        store_kernel,
        out_shape=(shape,) * 4,
        in_specs=[hbm] * 4,
        out_specs=(hbm,) * 4,
        scratch_shapes=[pltpu.VMEM((4, tokens, width), jnp.bfloat16), dma((2, 4))],
        compiler_params=pltpu.CompilerParams(vmem_limit_bytes=VMEM_LIMIT),
    )(*results)


def solution(mesh):
    split = P(("groups", "view"), None)
    return jax.shard_map(
        functools.partial(body, mesh.shape["view"]),
        mesh=mesh,
        in_specs=(split,) * 4 + (P("groups", None, None, None),),
        out_specs=(split,) * 4,
        check_vma=False,
    )
```

```python
import functools
import math

import jax
import jax.numpy as jnp
from jax import lax
from jax.experimental import pallas as pl
from jax.experimental.pallas import tpu as pltpu
from jax.sharding import PartitionSpec as P

H = 8
SPAN = 2
NEG_FILL = -1e30

PARTNER, RELAY, SIBLING, PASSED, OWN = range(5)
BLOCKS = 2 * SPAN + 1
VMEM_LIMIT = 60 * 1024 * 1024

AHEAD = 4

RELAYED, READY, SUMMED, RETURNED, DONE = 3, 5, 7, 11, 15


def kernel(
    devices,
    q_hbm,
    k_hbm,
    v_hbm,
    do_hbm,
    margin_ref,
    att_hbm,
    gq_hbm,
    gk_hbm,
    gv_hbm,
    q_ref,
    do_ref,
    att_ref,
    gq_ref,
    gk_ref,
    gv_ref,
    kv,
    acc,
    bias,
    out_buf,
    in_buf,
    load_sem,
    store_sem,
    kv_load,
    kv_send,
    kv_recv,
    pass_send,
    g_send,
    g_recv,
):
    tokens, width = q_hbm.shape
    dim = width // H
    scale = 1.0 / math.sqrt(dim)
    me = lax.axis_index("view")
    core = lax.rem(me, 2)
    chip = me // 2
    odd = lax.rem(chip, 2)
    sign = 1 - 2 * odd
    sibling = me + 1 - 2 * core
    partner = me + 2 * sign
    onward = lax.rem(me + 4 * sign + devices, devices)
    source = lax.rem(me - 4 * sign + devices, devices)
    shared = lax.rem(odd + core, 2)

    def cols(h):
        return pl.ds(pl.multiple_of(h * dim, dim), dim)

    def rows(block):
        return pl.ds(block * tokens, tokens)

    def send(src, dst, send_sem, recv_sem, to):
        return pltpu.make_async_remote_copy(
            src_ref=src,
            dst_ref=dst,
            send_sem=send_sem,
            recv_sem=recv_sem,
            device_id={"view": to},
            device_id_type=pl.DeviceIdType.MESH,
        )

    def load(h, part):
        return pltpu.make_async_copy(
            (k_hbm, v_hbm)[part].at[:, cols(h)], kv.at[h, part, rows(OWN), :], kv_load.at[part, h]
        )

    def store(h, n):
        return pltpu.make_async_copy(
            (att_ref, gq_ref, gk_ref, gv_ref)[n].at[:, cols(h)],
            (att_hbm, gq_hbm, gk_hbm, gv_hbm)[n].at[:, cols(h)],
            store_sem.at[n, h],
        )

    def first(h, block, to):
        return send(
            kv.at[h, :, rows(OWN), :],
            kv.at[h, :, rows(block), :],
            kv_send.at[block, h],
            kv_recv.at[block, h],
            to,
        )

    def relay(h):
        return send(
            kv.at[h, :, rows(PARTNER), :],
            kv.at[h, :, rows(RELAY), :],
            pass_send.at[0, h],
            kv_recv.at[RELAY, h],
            onward,
        )

    def forward(h, block):
        return send(
            kv.at[h, :, rows(block), :],
            kv.at[h, :, rows(PASSED), :],
            pass_send.at[1, h],
            kv_recv.at[PASSED, h],
            sibling,
        )

    def grad(h, block, to):
        return send(
            out_buf.at[h, block],
            in_buf.at[h, block],
            g_send.at[block, h],
            g_recv.at[block, h],
            to,
        )

    loads = (
        pltpu.make_async_copy(q_hbm, q_ref, load_sem.at[0]),
        pltpu.make_async_copy(do_hbm, do_ref, load_sem.at[1]),
    )
    barrier = pltpu.get_barrier_semaphore()
    for peer in (sibling, partner, onward, source):
        pl.semaphore_signal(
            barrier, inc=1, device_id={"view": peer}, device_id_type=pl.DeviceIdType.MESH
        )
    for h in range(H):
        for part in range(2):
            load(h, part).start()
    for copy in loads:
        copy.start()
    side = 1 - 2 * core
    order = (2 * sign, -2 * sign, side, -side)
    for block, offset in enumerate(order):
        place = offset + SPAN - (offset + SPAN) // (SPAN + 1)
        mask = margin_ref[place, me].astype(jnp.float32)
        bias[:, block * tokens : (block + 1) * tokens] = jnp.full(
            (8, tokens), (1.0 - mask) * NEG_FILL, jnp.float32
        )
    bias[:, OWN * tokens :] = jnp.zeros((8, tokens), jnp.float32)
    pl.semaphore_wait(barrier, 4)

    def launch(h):
        for part in range(2):
            load(h, part).wait()
        first(h, PARTNER, partner).start()
        first(h, SIBLING, sibling).start()

    for h in range(AHEAD):
        launch(h)
    for copy in loads:
        copy.wait()

    def dot(a, b, ca, cb):
        return lax.dot_general(a, b, (((ca,), (cb,)), ((), ())), preferred_element_type=jnp.float32)

    def compute(h):
        q = q_ref[:, cols(h)]
        do = do_ref[:, cols(h)]
        k_all = kv[h, 0]
        v_all = kv[h, 1]
        scores = dot(q, k_all, 1, 1) * scale + bias[0:1, :]
        e = jnp.exp(scores - jnp.max(scores, axis=-1, keepdims=True))
        prob = e * (1.0 / jnp.sum(e, axis=-1, keepdims=True))
        prob_half = prob.astype(jnp.bfloat16)
        att = dot(prob_half, v_all, 1, 0).astype(jnp.bfloat16)
        att_ref[:, cols(h)] = att
        row_dot = jnp.sum(
            do.astype(jnp.float32) * att.astype(jnp.float32), axis=-1, keepdims=True
        )
        prob_grad = dot(do, v_all, 1, 1)
        grad_half = (prob * (prob_grad - row_dot)).astype(jnp.bfloat16)
        gq_ref[:, cols(h)] = (dot(grad_half, k_all, 1, 0) * scale).astype(jnp.bfloat16)
        acc[h, 0] = dot(grad_half, q, 0, 0)
        acc[h, 1] = dot(prob_half, do, 0, 0)

    @pl.loop(0, H + DONE)
    def _(t):
        @pl.when(t < H)
        def _():
            first(t, PARTNER, partner).wait_recv()
            relay(t).start()

            @pl.when(t + AHEAD < H)
            def _():
                launch(t + AHEAD)

            @pl.when(shared == PARTNER)
            def _():
                forward(t, PARTNER).start()

        @pl.when((t >= RELAYED) & (t < H + RELAYED))
        def _():
            h = t - RELAYED
            relay(h).wait_recv()

            @pl.when(shared == RELAY)
            def _():
                forward(h, RELAY).start()

        @pl.when((t >= READY) & (t < H + READY))
        def _():
            h = t - READY
            first(h, SIBLING, sibling).wait_recv()
            forward(h, PARTNER).wait_recv()
            compute(h)
            for block in (PASSED, SIBLING):
                out_buf[h, block] = acc[h, :, block * tokens : (block + 1) * tokens, :].astype(
                    jnp.bfloat16
                )
                grad(h, block, sibling).start()
            store(h, 0).start()
            store(h, 1).start()

        @pl.when((t >= SUMMED) & (t < H + SUMMED))
        def _():
            h = t - SUMMED
            grad(h, PASSED, sibling).wait_recv()
            place = pl.ds(pl.multiple_of(shared * tokens, tokens), tokens)
            acc[h, :, place, :] += in_buf[h, PASSED].astype(jnp.float32)
            out_buf[h, RELAY] = acc[h, :, RELAY * tokens : (RELAY + 1) * tokens, :].astype(
                jnp.bfloat16
            )
            grad(h, RELAY, source).start()

        @pl.when((t >= RETURNED) & (t < H + RETURNED))
        def _():
            h = t - RETURNED
            grad(h, RELAY, source).wait_recv()
            out_buf[h, PARTNER] = (
                acc[h, :, :tokens, :] + in_buf[h, RELAY].astype(jnp.float32)
            ).astype(jnp.bfloat16)
            grad(h, PARTNER, partner).start()

        @pl.when(t >= DONE)
        def _():
            h = t - DONE
            grad(h, SIBLING, sibling).wait_recv()
            grad(h, PARTNER, partner).wait_recv()
            total = (
                acc[h, :, OWN * tokens :, :]
                + in_buf[h, SIBLING].astype(jnp.float32)
                + in_buf[h, PARTNER].astype(jnp.float32)
            )
            gk_ref[:, cols(h)] = (total[0] * scale).astype(jnp.bfloat16)
            gv_ref[:, cols(h)] = total[1].astype(jnp.bfloat16)
            store(h, 2).start()
            store(h, 3).start()

    @pl.loop(0, H)
    def _(h):
        first(h, PARTNER, partner).wait_send()
        first(h, SIBLING, sibling).wait_send()
        relay(h).wait_send()
        forward(h, PARTNER).wait_send()
        grad(h, PASSED, sibling).wait_send()
        grad(h, SIBLING, sibling).wait_send()
        grad(h, RELAY, source).wait_send()
        grad(h, PARTNER, partner).wait_send()
        for n in range(4):
            store(h, n).wait()


def store_kernel(*refs):
    sources, targets, held, sem = refs[:4], refs[4:8], refs[8], refs[9]
    fetches = [
        pltpu.make_async_copy(sources[n], held.at[n], sem.at[0, n]) for n in range(4)
    ]
    stores = [
        pltpu.make_async_copy(held.at[n], targets[n], sem.at[1, n]) for n in range(4)
    ]
    for fetch in fetches:
        fetch.start()
    for fetch, store in zip(fetches, stores):
        fetch.wait()
        store.start()
    for store in stores:
        store.wait()


def body(devices, query, keys, values, grad_out, margin):
    tokens, width = query.shape
    dim = width // H
    hbm = pl.BlockSpec(memory_space=pltpu.HBM)
    shape = jax.ShapeDtypeStruct((tokens, width), jnp.bfloat16)
    dma = pltpu.SemaphoreType.DMA
    results = pl.pallas_call(
        functools.partial(kernel, devices),
        out_shape=(shape,) * 4,
        in_specs=[hbm] * 4 + [pl.BlockSpec(memory_space=pltpu.SMEM)],
        out_specs=(hbm,) * 4,
        scratch_shapes=[
            *[pltpu.VMEM((tokens, width), jnp.bfloat16)] * 6,
            pltpu.VMEM((H, 2, BLOCKS * tokens, dim), jnp.bfloat16),
            pltpu.VMEM((H, 2, BLOCKS * tokens, dim), jnp.float32),
            pltpu.VMEM((8, BLOCKS * tokens), jnp.float32),
            pltpu.VMEM((H, 4, 2, tokens, dim), jnp.bfloat16),
            pltpu.VMEM((H, 4, 2, tokens, dim), jnp.bfloat16),
            dma((2,)),
            dma((4, H)),
            dma((2, H)),
            dma((4, H)),
            dma((4, H)),
            dma((2, H)),
            dma((4, H)),
            dma((4, H)),
        ],
        compiler_params=pltpu.CompilerParams(
            collective_id=0, has_side_effects=True, vmem_limit_bytes=VMEM_LIMIT
        ),
    )(query, keys, values, grad_out, margin.reshape(margin.shape[:2]).T)
    return pl.pallas_call(
        store_kernel,
        out_shape=(shape,) * 4,
        in_specs=[hbm] * 4,
        out_specs=(hbm,) * 4,
        scratch_shapes=[pltpu.VMEM((4, tokens, width), jnp.bfloat16), dma((2, 4))],
        compiler_params=pltpu.CompilerParams(vmem_limit_bytes=VMEM_LIMIT),
    )(*results)


def solution(mesh):
    split = P(("groups", "view"), None)
    return jax.shard_map(
        functools.partial(body, mesh.shape["view"]),
        mesh=mesh,
        in_specs=(split,) * 4 + (P("groups", None, None, None),),
        out_specs=(split,) * 4,
        check_vma=False,
    )
```

```python
import functools
import math

import jax
import jax.numpy as jnp
from jax import lax
from jax.experimental import pallas as pl
from jax.experimental.pallas import tpu as pltpu
from jax.sharding import PartitionSpec as P

H = 8
SPAN = 2
NEG_FILL = -1e30

PARTNER, RELAY, SIBLING, PASSED, OWN = range(5)
BLOCKS = 2 * SPAN + 1
VMEM_LIMIT = 60 * 1024 * 1024

AHEAD = 6

RELAYED, READY, SUMMED, RETURNED, DONE = 4, 6, 8, 12, 16


def kernel(
    devices,
    q_hbm,
    k_hbm,
    v_hbm,
    do_hbm,
    margin_ref,
    att_hbm,
    gq_hbm,
    gk_hbm,
    gv_hbm,
    q_ref,
    do_ref,
    att_ref,
    gq_ref,
    gk_ref,
    gv_ref,
    kv,
    acc,
    bias,
    out_buf,
    in_buf,
    load_sem,
    store_sem,
    kv_load,
    kv_send,
    kv_recv,
    pass_send,
    g_send,
    g_recv,
):
    tokens, width = q_hbm.shape
    dim = width // H
    scale = 1.0 / math.sqrt(dim)
    me = lax.axis_index("view")
    core = lax.rem(me, 2)
    chip = me // 2
    odd = lax.rem(chip, 2)
    sign = 1 - 2 * odd
    sibling = me + 1 - 2 * core
    partner = me + 2 * sign
    onward = lax.rem(me + 4 * sign + devices, devices)
    source = lax.rem(me - 4 * sign + devices, devices)
    shared = lax.rem(odd + core, 2)

    def cols(h):
        return pl.ds(pl.multiple_of(h * dim, dim), dim)

    def rows(block):
        return pl.ds(block * tokens, tokens)

    def send(src, dst, send_sem, recv_sem, to):
        return pltpu.make_async_remote_copy(
            src_ref=src,
            dst_ref=dst,
            send_sem=send_sem,
            recv_sem=recv_sem,
            device_id={"view": to},
            device_id_type=pl.DeviceIdType.MESH,
        )

    def load(h, part):
        return pltpu.make_async_copy(
            (k_hbm, v_hbm)[part].at[:, cols(h)], kv.at[h, part, rows(OWN), :], kv_load.at[part, h]
        )

    def store(h, n):
        return pltpu.make_async_copy(
            (att_ref, gq_ref, gk_ref, gv_ref)[n].at[:, cols(h)],
            (att_hbm, gq_hbm, gk_hbm, gv_hbm)[n].at[:, cols(h)],
            store_sem.at[n, h],
        )

    def first(h, block, to):
        return send(
            kv.at[h, :, rows(OWN), :],
            kv.at[h, :, rows(block), :],
            kv_send.at[block, h],
            kv_recv.at[block, h],
            to,
        )

    def relay(h):
        return send(
            kv.at[h, :, rows(PARTNER), :],
            kv.at[h, :, rows(RELAY), :],
            pass_send.at[0, h],
            kv_recv.at[RELAY, h],
            onward,
        )

    def forward(h, block):
        return send(
            kv.at[h, :, rows(block), :],
            kv.at[h, :, rows(PASSED), :],
            pass_send.at[1, h],
            kv_recv.at[PASSED, h],
            sibling,
        )

    def grad(h, block, to):
        return send(
            out_buf.at[h, block],
            in_buf.at[h, block],
            g_send.at[block, h],
            g_recv.at[block, h],
            to,
        )

    loads = (
        pltpu.make_async_copy(q_hbm, q_ref, load_sem.at[0]),
        pltpu.make_async_copy(do_hbm, do_ref, load_sem.at[1]),
    )
    barrier = pltpu.get_barrier_semaphore()
    for peer in (sibling, partner, onward, source):
        pl.semaphore_signal(
            barrier, inc=1, device_id={"view": peer}, device_id_type=pl.DeviceIdType.MESH
        )
    for h in range(H):
        for part in range(2):
            load(h, part).start()
    for copy in loads:
        copy.start()
    side = 1 - 2 * core
    order = (2 * sign, -2 * sign, side, -side)
    for block, offset in enumerate(order):
        place = offset + SPAN - (offset + SPAN) // (SPAN + 1)
        mask = margin_ref[place, me].astype(jnp.float32)
        bias[:, block * tokens : (block + 1) * tokens] = jnp.full(
            (8, tokens), (1.0 - mask) * NEG_FILL, jnp.float32
        )
    bias[:, OWN * tokens :] = jnp.zeros((8, tokens), jnp.float32)
    pl.semaphore_wait(barrier, 4)

    def launch(h):
        for part in range(2):
            load(h, part).wait()
        first(h, PARTNER, partner).start()
        first(h, SIBLING, sibling).start()

    for h in range(AHEAD):
        launch(h)
    for copy in loads:
        copy.wait()

    def dot(a, b, ca, cb):
        return lax.dot_general(a, b, (((ca,), (cb,)), ((), ())), preferred_element_type=jnp.float32)

    def compute(h):
        q = q_ref[:, cols(h)]
        do = do_ref[:, cols(h)]
        k_all = kv[h, 0]
        v_all = kv[h, 1]
        scores = dot(q, k_all, 1, 1) * scale + bias[0:1, :]
        e = jnp.exp(scores - jnp.max(scores, axis=-1, keepdims=True))
        prob = e * (1.0 / jnp.sum(e, axis=-1, keepdims=True))
        prob_half = prob.astype(jnp.bfloat16)
        att = dot(prob_half, v_all, 1, 0).astype(jnp.bfloat16)
        att_ref[:, cols(h)] = att
        row_dot = jnp.sum(
            do.astype(jnp.float32) * att.astype(jnp.float32), axis=-1, keepdims=True
        )
        prob_grad = dot(do, v_all, 1, 1)
        grad_half = (prob * (prob_grad - row_dot)).astype(jnp.bfloat16)
        gq_ref[:, cols(h)] = (dot(grad_half, k_all, 1, 0) * scale).astype(jnp.bfloat16)
        acc[h, 0] = dot(grad_half, q, 0, 0)
        acc[h, 1] = dot(prob_half, do, 0, 0)

    @pl.loop(0, H + DONE)
    def _(t):
        @pl.when(t < H)
        def _():
            first(t, PARTNER, partner).wait_recv()
            relay(t).start()

            @pl.when(t + AHEAD < H)
            def _():
                launch(t + AHEAD)

            @pl.when(shared == PARTNER)
            def _():
                forward(t, PARTNER).start()

        @pl.when((t >= RELAYED) & (t < H + RELAYED))
        def _():
            h = t - RELAYED
            relay(h).wait_recv()

            @pl.when(shared == RELAY)
            def _():
                forward(h, RELAY).start()

        @pl.when((t >= READY) & (t < H + READY))
        def _():
            h = t - READY
            first(h, SIBLING, sibling).wait_recv()
            forward(h, PARTNER).wait_recv()
            compute(h)
            for block in (PASSED, SIBLING):
                out_buf[h, block] = acc[h, :, block * tokens : (block + 1) * tokens, :].astype(
                    jnp.bfloat16
                )
                grad(h, block, sibling).start()
            store(h, 0).start()
            store(h, 1).start()

        @pl.when((t >= SUMMED) & (t < H + SUMMED))
        def _():
            h = t - SUMMED
            grad(h, PASSED, sibling).wait_recv()
            place = pl.ds(pl.multiple_of(shared * tokens, tokens), tokens)
            acc[h, :, place, :] += in_buf[h, PASSED].astype(jnp.float32)
            out_buf[h, RELAY] = acc[h, :, RELAY * tokens : (RELAY + 1) * tokens, :].astype(
                jnp.bfloat16
            )
            grad(h, RELAY, source).start()

        @pl.when((t >= RETURNED) & (t < H + RETURNED))
        def _():
            h = t - RETURNED
            grad(h, RELAY, source).wait_recv()
            out_buf[h, PARTNER] = (
                acc[h, :, :tokens, :] + in_buf[h, RELAY].astype(jnp.float32)
            ).astype(jnp.bfloat16)
            grad(h, PARTNER, partner).start()

        @pl.when(t >= DONE)
        def _():
            h = t - DONE
            grad(h, SIBLING, sibling).wait_recv()
            grad(h, PARTNER, partner).wait_recv()
            total = (
                acc[h, :, OWN * tokens :, :]
                + in_buf[h, SIBLING].astype(jnp.float32)
                + in_buf[h, PARTNER].astype(jnp.float32)
            )
            gk_ref[:, cols(h)] = (total[0] * scale).astype(jnp.bfloat16)
            gv_ref[:, cols(h)] = total[1].astype(jnp.bfloat16)
            store(h, 2).start()
            store(h, 3).start()

    @pl.loop(0, H)
    def _(h):
        first(h, PARTNER, partner).wait_send()
        first(h, SIBLING, sibling).wait_send()
        relay(h).wait_send()
        forward(h, PARTNER).wait_send()
        grad(h, PASSED, sibling).wait_send()
        grad(h, SIBLING, sibling).wait_send()
        grad(h, RELAY, source).wait_send()
        grad(h, PARTNER, partner).wait_send()
        for n in range(4):
            store(h, n).wait()


def store_kernel(*refs):
    sources, targets, held, sem = refs[:4], refs[4:8], refs[8], refs[9]
    fetches = [
        pltpu.make_async_copy(sources[n], held.at[n], sem.at[0, n]) for n in range(4)
    ]
    stores = [
        pltpu.make_async_copy(held.at[n], targets[n], sem.at[1, n]) for n in range(4)
    ]
    for fetch in fetches:
        fetch.start()
    for fetch, store in zip(fetches, stores):
        fetch.wait()
        store.start()
    for store in stores:
        store.wait()


def body(devices, query, keys, values, grad_out, margin):
    tokens, width = query.shape
    dim = width // H
    hbm = pl.BlockSpec(memory_space=pltpu.HBM)
    shape = jax.ShapeDtypeStruct((tokens, width), jnp.bfloat16)
    dma = pltpu.SemaphoreType.DMA
    results = pl.pallas_call(
        functools.partial(kernel, devices),
        out_shape=(shape,) * 4,
        in_specs=[hbm] * 4 + [pl.BlockSpec(memory_space=pltpu.SMEM)],
        out_specs=(hbm,) * 4,
        scratch_shapes=[
            *[pltpu.VMEM((tokens, width), jnp.bfloat16)] * 6,
            pltpu.VMEM((H, 2, BLOCKS * tokens, dim), jnp.bfloat16),
            pltpu.VMEM((H, 2, BLOCKS * tokens, dim), jnp.float32),
            pltpu.VMEM((8, BLOCKS * tokens), jnp.float32),
            pltpu.VMEM((H, 4, 2, tokens, dim), jnp.bfloat16),
            pltpu.VMEM((H, 4, 2, tokens, dim), jnp.bfloat16),
            dma((2,)),
            dma((4, H)),
            dma((2, H)),
            dma((4, H)),
            dma((4, H)),
            dma((2, H)),
            dma((4, H)),
            dma((4, H)),
        ],
        compiler_params=pltpu.CompilerParams(
            collective_id=0, has_side_effects=True, vmem_limit_bytes=VMEM_LIMIT
        ),
    )(query, keys, values, grad_out, margin.reshape(margin.shape[:2]).T)
    return pl.pallas_call(
        store_kernel,
        out_shape=(shape,) * 4,
        in_specs=[hbm] * 4,
        out_specs=(hbm,) * 4,
        scratch_shapes=[pltpu.VMEM((4, tokens, width), jnp.bfloat16), dma((2, 4))],
        compiler_params=pltpu.CompilerParams(vmem_limit_bytes=VMEM_LIMIT),
    )(*results)


def solution(mesh):
    split = P(("groups", "view"), None)
    return jax.shard_map(
        functools.partial(body, mesh.shape["view"]),
        mesh=mesh,
        in_specs=(split,) * 4 + (P("groups", None, None, None),),
        out_specs=(split,) * 4,
        check_vma=False,
    )
```
